32 devices in a mesh: dp: 4 (over y, x), expert: 4 (over z), tensor: 2 (over core).
Axes of the slice: x: 2, y: 2, z: 4, core: 2. Of those that a mesh axis runs over, the one named last changes fastest.
Arguments:
- tokens: bfloat16 [2048, 2048], P(('dp', 'expert')), may hold values from -6 to 6
- expert_ids: int32 [2048, 8], P(('dp', 'expert')), may hold values from 0 to 15, as said below
- gates: float32 [2048, 8], P(('dp', 'expert')), may hold values from 0.05 to 0.5
- token_weight: float32 [2048], P(('dp', 'expert')), may hold values from 0.25 to 4
- w_gate: bfloat16 [16, 2048, 768], P(('dp', 'expert'), None, 'tensor'), may hold values from -0.125 to 0.125
- w_up: bfloat16 [16, 2048, 768], P(('dp', 'expert'), None, 'tensor'), may hold values from -0.125 to 0.125
- w_down: bfloat16 [16, 768, 2048], P(('dp', 'expert'), 'tensor'), may hold values from -0.21875 to 0.21875
- v_gate: bfloat16 [16, 2048, 768], P(('dp', 'expert'), None, 'tensor'), may hold values from -0.125 to 0.125
- v_up: bfloat16 [16, 2048, 768], P(('dp', 'expert'), None, 'tensor'), may hold values from -0.125 to 0.125
- v_down: bfloat16 [16, 768, 2048], P(('dp', 'expert'), 'tensor'), may hold values from -0.21875 to 0.21875
Outputs:
- gv_gate: float32 [16, 2048, 768], P(('dp', 'expert'), None, 'tensor')
- gv_up: float32 [16, 2048, 768], P(('dp', 'expert'), None, 'tensor')
- gv_down: float32 [16, 768, 2048], P(('dp', 'expert'), 'tensor')
- tangent: bfloat16 [2048, 2048], P(('dp', 'expert'), 'tensor')
The draws below stay inside these ranges and needn't reach their ends.
Inputs may be any that keep to these rules, and one draw needn't show every extreme that they name: `expert_ids`: each row names 8 different experts. Among the 128 rows of one index of dp and expert (aligned blocks of rows) no expert is named more than 128 times, and one expert is named exactly 128 times by the rows of every such block.
All inputs are finite; a program needn't handle non-finite values.
Results may differ from the reference program's by a relative error of at most 0.0063.
Values may be sent and summed in bfloat16 or wider, within the bound.
A program may use at most 256 MiB of HBM per device.

```python
import math
import jax
import jax.numpy as jnp
from jax import lax

D = 2048
H = 768
TOPK = 8
BLOCK = 128
TOK_DEV = 128
EXPERTS = 16
TOKENS = 2048
CAP = 128
N_TENSOR = 2


def block_choices(key, hot, share):
    others = EXPERTS - 1
    extra = CAP - share
    base = extra // others
    rest = extra % others
    key_order, key_mix, key_swing, key_tokens = jax.random.split(key, 4)
    order = jax.random.permutation(key_order, others).astype(jnp.int32)
    labels = order + (order >= hot).astype(jnp.int32)
    cuts = base + (jnp.arange(others) < rest).astype(jnp.int32)
    quota = jnp.full((EXPERTS,), share, jnp.int32)
    quota = quota.at[labels].add(-cuts)
    quota = quota.at[hot].set(CAP)
    pairs = others // 2
    mixed = jax.random.permutation(key_mix, others).astype(jnp.int32)
    mixed = mixed + (mixed >= hot).astype(jnp.int32)
    swing = jax.random.randint(key_swing, (pairs,), 0, share // 2 + 1).astype(jnp.int32)
    quota = quota.at[mixed[0:2 * pairs:2]].add(swing)
    quota = quota.at[mixed[1:2 * pairs:2]].add(-swing)
    ends = jnp.cumsum(quota)
    spots = jnp.arange(TOK_DEV * TOPK, dtype=jnp.int32)
    sequence = jnp.sum((spots[:, None] >= ends[None, :]).astype(jnp.int32), axis=1)
    chosen = sequence.reshape(TOPK, TOK_DEV).T
    shuffle = jax.random.permutation(key_tokens, TOK_DEV)
    return chosen[shuffle]


def draw_expert_ids(key, part):
    key = jax.random.fold_in(key, 11)
    blocks = TOKENS // TOK_DEV
    share = TOK_DEV * TOPK // EXPERTS
    hot = jax.random.randint(jax.random.fold_in(key, 1), (), 0, EXPERTS).astype(jnp.int32)
    keys = jax.random.split(jax.random.fold_in(key, 2), blocks)
    chosen = jax.vmap(lambda block_key: block_choices(block_key, hot, share))(keys)
    return chosen.reshape(TOKENS, TOPK).astype(jnp.int32)


def block_scale(own_key, extent, pieces, least, high):
    loudness = 1.0
    for position, shards_of in pieces:
        steps = jax.random.uniform(jax.random.fold_in(jax.random.fold_in(own_key, 6), position), (shards_of,), jnp.float32, least / len(pieces), high / len(pieces))
        loudness = loudness * jnp.repeat(jnp.exp(steps), extent[position] // shards_of).reshape((-1,) + (1,) * (len(extent) - 1 - position))
    return loudness


def bell_draw(rng, dims, deviation, limit, pieces=(), kind=jnp.bfloat16):
    factor_of = block_scale(rng, dims, pieces, -0.22, 0.18) if pieces else 1.0
    result = jax.random.normal(rng, dims, jnp.float32) * deviation * factor_of
    return jnp.minimum(jnp.maximum(result, -limit), limit).astype(kind)


def setup_inputs(seed: int = 0) -> dict:
    streams_of = jax.random.split(jax.random.key(seed), 11)
    tokens = bell_draw(streams_of[0], (TOKENS, D), 1.0, 6.0, ((0, 16),))
    expert_ids = draw_expert_ids(jax.random.fold_in(streams_of[10], 71), 0)
    gates = jnp.clip(0.05 + 0.45 * jax.random.uniform(streams_of[2], (TOKENS, TOPK), jnp.float32) ** block_scale(streams_of[2], (TOKENS, TOPK), ((0, 16),), -0.2, 0.2), 0.05, 0.5)
    token_weight = jnp.clip(jnp.exp(math.log(4.0) - 2.7725887 * jax.random.uniform(streams_of[3], (TOKENS,), jnp.float32) ** block_scale(streams_of[3], (TOKENS,), ((0, 16),), -0.2, 0.2)), 0.25, 4.0)
    w_gate = bell_draw(streams_of[4], (EXPERTS, D, H), D ** -0.5, 0.125, ((0, 16), (2, 2)))
    w_up = bell_draw(streams_of[5], (EXPERTS, D, H), D ** -0.5, 0.125, ((0, 16), (2, 2)))
    w_down = bell_draw(streams_of[6], (EXPERTS, H, D), H ** -0.5, 0.21875, ((0, 16), (1, 2)))
    v_gate = bell_draw(streams_of[7], (EXPERTS, D, H), D ** -0.5, 0.125, ((0, 16), (2, 2)))
    v_up = bell_draw(streams_of[8], (EXPERTS, D, H), D ** -0.5, 0.125, ((0, 16), (2, 2)))
    v_down = bell_draw(streams_of[9], (EXPERTS, H, D), H ** -0.5, 0.21875, ((0, 16), (1, 2)))
    return {"tokens": tokens, "expert_ids": expert_ids, "gates": gates, "token_weight": token_weight, "w_gate": w_gate, "w_up": w_up, "w_down": w_down, "v_gate": v_gate, "v_up": v_up, "v_down": v_down}


def silu_parts(pre_gate):
    sigma = jax.nn.sigmoid(pre_gate)
    return pre_gate * sigma, sigma * (1.0 + pre_gate * (1.0 - sigma))


def expert_layout(expert_ids):
    flat = expert_ids.reshape(-1).astype(jnp.int32)
    order = jnp.argsort(flat, stable=True).astype(jnp.int32)
    labels = jnp.arange(EXPERTS, dtype=jnp.int32)
    counts = jnp.sum((flat[:, None] == labels[None, :]).astype(jnp.int32), axis=0)
    starts = jnp.cumsum(counts) - counts
    return order, counts, starts


def block_rows(order, counts, starts, expert, number):
    offsets = number * BLOCK + jnp.arange(BLOCK, dtype=jnp.int32)
    valid = offsets < counts[expert]
    spots = jnp.clip(starts[expert] + offsets, 0, order.shape[0] - 1)
    flat_rows = jnp.where(valid, order[spots], 0).astype(jnp.int32)
    return flat_rows, valid


def reference(tokens, expert_ids, gates, token_weight, w_gate, w_up, w_down, v_gate, v_up, v_down):
    order, counts, starts = expert_layout(expert_ids)
    flat_gates = gates.reshape(-1)
    half = H // N_TENSOR
    zero_bf = jnp.zeros((), jnp.bfloat16)

    def gather_x(flat_rows, valid):
        owners = flat_rows // TOPK
        rows_x = jnp.where(valid[:, None], tokens[owners], zero_bf).astype(jnp.bfloat16)
        weight = jnp.where(valid, flat_gates[flat_rows], 0.0).astype(jnp.float32)
        return owners, rows_x, weight

    def forward_expert(carry, expert):
        def one_block(number, total):
            flat_rows, valid = block_rows(order, counts, starts, expert, number)
            owners, rows_x, weight = gather_x(flat_rows, valid)
            pre_gate = jnp.dot(rows_x, w_gate[expert], preferred_element_type=jnp.float32)
            pre_up = jnp.dot(rows_x, w_up[expert], preferred_element_type=jnp.float32)
            d_gate = jnp.dot(rows_x, v_gate[expert], preferred_element_type=jnp.float32)
            d_up = jnp.dot(rows_x, v_up[expert], preferred_element_type=jnp.float32)
            silu_g, slope_g = silu_parts(pre_gate)
            act = (silu_g * pre_up).astype(jnp.bfloat16)
            d_act = (slope_g * d_gate * pre_up + silu_g * d_up).astype(jnp.bfloat16)
            act_split = act.astype(jnp.float32).reshape(BLOCK, N_TENSOR, half)
            dact_split = d_act.astype(jnp.float32).reshape(BLOCK, N_TENSOR, half)
            down_split = w_down[expert].astype(jnp.float32).reshape(N_TENSOR, half, D)
            vdown_split = v_down[expert].astype(jnp.float32).reshape(N_TENSOR, half, D)
            parts = jnp.einsum("bnh,nhd->bnd", dact_split, down_split) + jnp.einsum("bnh,nhd->bnd", act_split, vdown_split)
            parts = lax.optimization_barrier(parts.astype(jnp.bfloat16)).astype(jnp.float32)
            row_sum = jnp.sum(parts, axis=1)
            return total.at[owners].add(weight[:, None] * row_sum)

        blocks = (counts[expert] + BLOCK - 1) // BLOCK
        return lax.fori_loop(0, blocks, one_block, carry), None

    dy, _ = lax.scan(forward_expert, jnp.zeros((TOKENS, D), jnp.float32), jnp.arange(EXPERTS, dtype=jnp.int32))
    tangent = dy.astype(jnp.bfloat16)
    scaled = token_weight[:, None] * dy
    factor = 1.0 / (TOK_DEV * TOPK) ** 0.5

    def backward_expert(expert):
        def one_block(number, sums):
            flat_rows, valid = block_rows(order, counts, starts, expert, number)
            owners, rows_x, weight = gather_x(flat_rows, valid)
            rows_q = (weight[:, None] * scaled[owners]).astype(jnp.bfloat16)
            pre_gate = jnp.dot(rows_x, w_gate[expert], preferred_element_type=jnp.float32)
            pre_up = jnp.dot(rows_x, w_up[expert], preferred_element_type=jnp.float32)
            silu_g, slope_g = silu_parts(pre_gate)
            act = (silu_g * pre_up).astype(jnp.bfloat16)
            back = jnp.dot(rows_q, w_down[expert].T, preferred_element_type=jnp.float32)
            grad_gate = (back * pre_up * slope_g).astype(jnp.bfloat16)
            grad_up = (back * silu_g).astype(jnp.bfloat16)
            return (sums[0] + jnp.dot(rows_x.T, grad_gate, preferred_element_type=jnp.float32),
                    sums[1] + jnp.dot(rows_x.T, grad_up, preferred_element_type=jnp.float32),
                    sums[2] + jnp.dot(act.T, rows_q, preferred_element_type=jnp.float32))

        start = (jnp.zeros((D, H), jnp.float32), jnp.zeros((D, H), jnp.float32), jnp.zeros((H, D), jnp.float32))
        blocks = (counts[expert] + BLOCK - 1) // BLOCK
        sums = lax.fori_loop(0, blocks, one_block, start)
        return (factor * sums[0], factor * sums[1], factor * sums[2])

    gv_gate, gv_up, gv_down = lax.map(backward_expert, jnp.arange(EXPERTS, dtype=jnp.int32))
    return gv_gate, gv_up, gv_down, tangent
```

```python
import functools

import jax
import jax.numpy as jnp
from jax import lax
from jax.experimental import pallas as pl
from jax.experimental.pallas import tpu as pltpu
from jax.sharding import PartitionSpec as P

MESH = pl.DeviceIdType.MESH
ANY = pl.BlockSpec(memory_space=pl.ANY)
AXES = ("dp", "expert")


def product(left, right):
    return jnp.dot(left, right, preferred_element_type=jnp.float32)


def contract_rows(left, right):
    return lax.dot_general(
        left, right, (((0,), (0,)), ((), ())), preferred_element_type=jnp.float32
    )


def silu_parts(pre_gate):
    sigma = jax.nn.sigmoid(pre_gate)
    return (pre_gate * sigma, sigma * (1.0 + pre_gate * (1.0 - sigma)))


def place():
    d, z, c = lax.axis_index("dp"), lax.axis_index("expert"), lax.axis_index("tensor")
    flip_low = d + 1 - 2 * (d % 2)
    flip_high = d + 2 - 4 * (d // 2)
    first = flip_low * (1 - c) + flip_high * c
    second = flip_high * (1 - c) + flip_low * c
    return d, z, c, first, second


def greet(depth):
    d, z, c, first, second = place()
    barrier = pltpu.get_barrier_semaphore()
    peers = [(d, (z + k) % depth, c) for k in range(1, depth)]
    peers += [(first, z, c), (second, z, c), (d, z, 1 - c)]
    for peer in peers:
        pl.semaphore_signal(barrier, inc=1, device_id=peer, device_id_type=MESH)
    pl.semaphore_wait(barrier, len(peers))


def push(src, dst, sems, row, col, peer):
    send, recv = sems
    copy = pltpu.make_async_remote_copy(
        src_ref=src, dst_ref=dst, send_sem=send.at[row, col], recv_sem=recv.at[row, col],
        device_id=peer, device_id_type=MESH,
    )
    copy.start()
    return copy


def spread(depth, src, out, sems, local_sem):
    d, z, c, first, second = place()
    to_first, to_second, to_core = (first, z, c), (second, z, c), (d, z, 1 - c)
    sent, along, one, two, three, cores = [], {}, {}, {}, {}, []
    spot = out.at[d * depth + z, c]
    keep = pltpu.make_async_copy(src, spot, local_sem)
    keep.start()
    for k in range(1, depth):
        along[k] = push(src, spot, sems, 0, k, (d, (z + k) % depth, c))
    for j in range(depth + 1):
        if j < depth:
            from_z = (z - j + depth) % depth
            here = out.at[d * depth + from_z, c]
            if j:
                along[j].wait_recv()
            body = here if j else src
            one[j] = push(body, here, sems, 1, j, to_first)
            two[j] = push(body, here, sems, 2, j, to_second)
            cores.append(push(body, here, sems, 4, j, to_core))
        if j >= 1:
            i = j - 1
            from_z = (z - i + depth) % depth
            one[i].wait_recv()
            here = out.at[first * depth + from_z, c]
            three[i] = push(here, here, sems, 3, i, to_second)
            cores.append(push(here, here, sems, 5, i, to_core))
            two[i].wait_recv()
            here = out.at[second * depth + from_z, c]
            cores.append(push(here, here, sems, 6, i, to_core))
    for j in range(depth):
        from_z = (z - j + depth) % depth
        three[j].wait_recv()
        here = out.at[(3 - d) * depth + from_z, c]
        cores.append(push(here, here, sems, 7, j, to_core))
    for copy in cores:
        copy.wait_recv()
    for group in (along, one, two, three):
        for copy in group.values():
            copy.wait_send()
    for copy in cores:
        copy.wait_send()
    keep.wait()


def gather_kernel(depth, x_ref, down_ref, vdown_ref, out_ref, mats_ref, send, recv, wsend, wrecv, local):
    d, z, c, _, _ = place()
    greet(depth)
    spread_src = x_ref.at[c]
    own = [
        pltpu.make_async_copy(down_ref, mats_ref.at[0], local.at[1]),
        pltpu.make_async_copy(vdown_ref, mats_ref.at[1], local.at[2]),
    ]
    for copy in own:
        copy.start()
    other = [
        push(down_ref, mats_ref.at[2], (wsend, wrecv), 0, 0, (d, z, 1 - c)),
        push(vdown_ref, mats_ref.at[3], (wsend, wrecv), 0, 1, (d, z, 1 - c)),
    ]
    spread(depth, spread_src, out_ref, (send, recv), local.at[0])
    for copy in own + other:
        copy.wait()


def add_rows(rows, store, *terms):
    step = 16

    @pl.loop(0, rows // step)
    def _(i):
        at = pl.ds(pl.multiple_of(i * step, step), step)
        total = terms[0][at, :].astype(jnp.float32)
        for term in terms[1:]:
            total = total + term[at, :].astype(jnp.float32)
        store[at, :] = total.astype(store.dtype)


def reduce_kernel(
    depth, part_ref, out_ref, land_a, mine, send_b, land_b, send_c, land_c, own, total,
    rsend, rrecv, load, send, recv, local,
):
    d, z, c, first, second = place()
    rows = total.shape[0]
    order = list(range(1, depth)) + [0]
    loads = {}
    for k in order:
        zt = (z + k) % depth
        for slot, chip in ((1, second), (0, d)):
            loads[k, slot] = pltpu.make_async_copy(
                part_ref.at[chip * depth + zt], mine.at[k, slot], load.at[k, slot]
            )
            loads[k, slot].start()
    greet(depth)
    hop, turn, last = {}, {}, {}
    for k in order:
        zt = (z + k) % depth
        for slot, chip in ((1, 3 - d), (0, first)):
            hop[k, slot] = push(
                part_ref.at[chip * depth + zt], land_a.at[k, slot], (rsend, rrecv), slot, k, (first, z, c)
            )

    def finish(k):
        hop[k, 0].wait_recv()
        loads[k, 0].wait()
        turn[k].wait_recv()
        if k:
            add_rows(rows, send_c.at[k], mine.at[k, 0], land_a.at[k, 0], land_b.at[k])
            last[k] = push(
                send_c.at[k], land_c.at[k], (rsend, rrecv), 3, k, (d, (z + k) % depth, c)
            )
        else:
            add_rows(rows, own, mine.at[k, 0], land_a.at[k, 0], land_b.at[k])

    for i, k in enumerate(order):
        hop[k, 1].wait_recv()
        loads[k, 1].wait()
        add_rows(rows, send_b.at[k], mine.at[k, 1], land_a.at[k, 1])
        turn[k] = push(send_b.at[k], land_b.at[k], (rsend, rrecv), 2, k, (second, z, c))
        if i:
            finish(order[i - 1])
    finish(order[-1])
    for k in range(1, depth):
        last[k].wait_recv()
    add_rows(rows, total, own, *[land_c.at[k] for k in range(1, depth)])
    spread(depth, total, out_ref, (send, recv), local.at[0])
    for group in (hop, turn, last):
        for copy in group.values():
            copy.wait_send()


def gather_tokens(tokens, down_mat, vdown_mat):
    depth = lax.axis_size("expert")
    groups = lax.axis_size("dp") * depth
    count, width = tokens.shape
    half = count // 2
    dma = pltpu.SemaphoreType.DMA
    return pl.pallas_call(
        functools.partial(gather_kernel, depth),
        out_shape=(
            jax.ShapeDtypeStruct((groups, 2, half, width), jnp.bfloat16),
            jax.ShapeDtypeStruct((4,) + down_mat.shape, jnp.bfloat16),
        ),
        in_specs=[ANY, ANY, ANY],
        out_specs=(ANY, ANY),
        scratch_shapes=[dma((8, depth)), dma((8, depth)), dma((1, 2)), dma((1, 2)), dma((3,))],
        compiler_params=pltpu.CompilerParams(collective_id=0, has_side_effects=True),
    )(tokens.reshape(2, half, width), down_mat, vdown_mat)


def reduce_and_spread(part):
    depth = lax.axis_size("expert")
    groups, rows, width = part.shape
    dma = pltpu.SemaphoreType.DMA
    buf = lambda *lead: pltpu.VMEM(lead + (rows, width), jnp.bfloat16)
    return pl.pallas_call(
        functools.partial(reduce_kernel, depth),
        out_shape=jax.ShapeDtypeStruct((groups, 2, rows, width), jnp.bfloat16),
        in_specs=[ANY],
        out_specs=ANY,
        scratch_shapes=[
            buf(depth, 2), buf(depth, 2), buf(depth), buf(depth), buf(depth), buf(depth),
            pltpu.VMEM((rows, width), jnp.float32), buf(),
            dma((4, depth)), dma((4, depth)), dma((depth, 2)),
            dma((8, depth)), dma((8, depth)), dma((1,)),
        ],
        compiler_params=pltpu.CompilerParams(
            collective_id=1, has_side_effects=True, vmem_limit_bytes=48 * 1024 * 1024
        ),
    )(part)


def body(tokens, expert_ids, gates, token_weight, w_gate, w_up, w_down, v_gate, v_up, v_down):
    tok_count, width = tokens.shape
    picks = expert_ids.shape[1]
    groups = lax.axis_size("dp") * lax.axis_size("expert")
    half_tok = tok_count // 2
    core = lax.axis_index("tensor")
    me = lax.axis_index("dp") * lax.axis_size("expert") + lax.axis_index("expert")
    labels = jnp.arange(groups, dtype=jnp.int32)
    dense = jnp.sum(
        jnp.where(expert_ids[:, :, None] == labels, gates[:, :, None], 0.0), axis=1
    )
    table = jnp.concatenate([dense, token_weight[:, None]], axis=1)
    table = lax.all_gather(table, AXES, axis=0, tiled=True)
    gate_of = lax.dynamic_slice_in_dim(table, me, 1, 1)
    scale_of = gate_of * table[:, groups:]

    x_parts, mats = gather_tokens(tokens, w_down[0], v_down[0])
    x = x_parts.reshape(groups * tok_count, width)
    pre_gate = product(x, w_gate[0])
    pre_up = product(x, w_up[0])
    d_gate = product(x, v_gate[0])
    d_up = product(x, v_up[0])
    silu_g, slope_g = silu_parts(pre_gate)
    act_wide = silu_g * pre_up
    act = act_wide.astype(jnp.bfloat16)
    d_act = (slope_g * d_gate * pre_up + silu_g * d_up).astype(jnp.bfloat16)

    hidden = act.shape[1]
    both = jnp.concatenate([d_act, act], axis=1).reshape(groups, 2, half_tok, 2 * hidden)
    keep = lax.dynamic_index_in_dim(both, core, 1, keepdims=False)
    give = lax.dynamic_index_in_dim(both, 1 - core, 1, keepdims=False)
    got = lax.ppermute(give, "tensor", [(0, 1), (1, 0)])
    left = jnp.concatenate([keep, got], axis=2).reshape(groups * half_tok, 4 * hidden)
    gate_half = lax.dynamic_index_in_dim(
        gate_of.reshape(groups, 2, half_tok), core, 1, keepdims=False
    ).reshape(groups * half_tok, 1)
    part = (gate_half * product(left, mats.reshape(4 * hidden, width))).astype(jnp.bfloat16)

    dy_parts = reduce_and_spread(part.reshape(groups, half_tok, width))
    dy = dy_parts.reshape(groups * tok_count, width)
    tangent = lax.dynamic_slice(
        dy, (me * tok_count, core * (width // 2)), (tok_count, width // 2)
    )
    back = scale_of * lax.dot_general(
        dy, w_down[0], (((1,), (1,)), ((), ())), preferred_element_type=jnp.float32
    )
    grad_gate = (back * pre_up * slope_g).astype(jnp.bfloat16)
    grad_up = (back * silu_g).astype(jnp.bfloat16)
    act_scaled = (scale_of * act_wide).astype(jnp.bfloat16)
    factor = 1.0 / (tok_count * picks) ** 0.5
    return (
        (factor * contract_rows(x, grad_gate))[None],
        (factor * contract_rows(x, grad_up))[None],
        (factor * contract_rows(act_scaled, dy))[None],
        tangent,
    )


def solution(mesh):
    rows = P(AXES, None)
    wide = P(AXES, None, "tensor")
    tall = P(AXES, "tensor", None)
    in_specs = (rows, rows, rows, P(AXES), wide, wide, tall, wide, wide, tall)
    out_specs = (wide, wide, tall, P(AXES, "tensor"))
    return jax.shard_map(body, mesh=mesh, in_specs=in_specs, out_specs=out_specs, check_vma=False)
```

```python
import functools

import jax
import jax.numpy as jnp
from jax import lax
from jax.experimental import pallas as pl
from jax.experimental.pallas import tpu as pltpu
from jax.sharding import PartitionSpec as P

MESH = pl.DeviceIdType.MESH
ANY = pl.BlockSpec(memory_space=pl.ANY)
AXES = ("dp", "expert")


def product(left, right):
    return jnp.dot(left, right, preferred_element_type=jnp.float32)


def contract_rows(left, right):
    return lax.dot_general(
        left, right, (((0,), (0,)), ((), ())), preferred_element_type=jnp.float32
    )


def silu_parts(pre_gate):
    sigma = jax.nn.sigmoid(pre_gate)
    return (pre_gate * sigma, sigma * (1.0 + pre_gate * (1.0 - sigma)))


def place():
    d, z, c = lax.axis_index("dp"), lax.axis_index("expert"), lax.axis_index("tensor")
    flip_low = d + 1 - 2 * (d % 2)
    flip_high = d + 2 - 4 * (d // 2)
    first = flip_low * (1 - c) + flip_high * c
    second = flip_high * (1 - c) + flip_low * c
    return d, z, c, first, second


def greet(depth):
    d, z, c, first, second = place()
    barrier = pltpu.get_barrier_semaphore()
    peers = [(d, (z + k) % depth, c) for k in range(1, depth)]
    peers += [(first, z, c), (second, z, c), (d, z, 1 - c)]
    for peer in peers:
        pl.semaphore_signal(barrier, inc=1, device_id=peer, device_id_type=MESH)
    pl.semaphore_wait(barrier, len(peers))


def push(src, dst, sems, row, col, peer):
    send, recv = sems
    copy = pltpu.make_async_remote_copy(
        src_ref=src, dst_ref=dst, send_sem=send.at[row, col], recv_sem=recv.at[row, col],
        device_id=peer, device_id_type=MESH,
    )
    copy.start()
    return copy


def spread(depth, src, out, sems, local_sem, small=None):
    d, z, c, first, second = place()
    to_first, to_second, to_core = (first, z, c), (second, z, c), (d, z, 1 - c)
    sent, along, one, two, three, cores = [], {}, {}, {}, {}, []
    spot = out.at[d * depth + z, c]
    keep = pltpu.make_async_copy(src, spot, local_sem)
    keep.start()
    extra, flat = {}, None
    if small is not None:
        flat, all_flat = small
        flat_spot = all_flat.at[d * depth + z]
        flat_keep = pltpu.make_async_copy(flat, flat_spot, local_sem)
    for k in range(1, depth):
        to_z = (d, (z + k) % depth, c)
        if flat is not None:
            extra[0, k] = push(flat, flat_spot, sems, 8, k, to_z)
        along[k] = push(src, spot, sems, 0, k, to_z)
    for j in range(depth + 1):
        if j < depth:
            from_z = (z - j + depth) % depth
            here = out.at[d * depth + from_z, c]
            if j:
                along[j].wait_recv()
            if flat is not None:
                if j:
                    extra[0, j].wait_recv()
                flat_here = all_flat.at[d * depth + from_z]
                flat_body = flat_here if j else flat
                extra[1, j] = push(flat_body, flat_here, sems, 9, j, to_first)
                extra[2, j] = push(flat_body, flat_here, sems, 10, j, to_second)
            body = here if j else src
            one[j] = push(body, here, sems, 1, j, to_first)
            two[j] = push(body, here, sems, 2, j, to_second)
            cores.append(push(body, here, sems, 4, j, to_core))
        if j >= 1:
            i = j - 1
            from_z = (z - i + depth) % depth
            one[i].wait_recv()
            here = out.at[first * depth + from_z, c]
            three[i] = push(here, here, sems, 3, i, to_second)
            if flat is not None:
                extra[1, i].wait_recv()
                flat_here = all_flat.at[first * depth + from_z]
                extra[3, i] = push(flat_here, flat_here, sems, 11, i, to_second)
            cores.append(push(here, here, sems, 5, i, to_core))
            two[i].wait_recv()
            here = out.at[second * depth + from_z, c]
            cores.append(push(here, here, sems, 6, i, to_core))
    for j in range(depth):
        from_z = (z - j + depth) % depth
        three[j].wait_recv()
        here = out.at[(3 - d) * depth + from_z, c]
        cores.append(push(here, here, sems, 7, j, to_core))
    for copy in cores:
        copy.wait_recv()
    for group in (along, one, two, three):
        for copy in group.values():
            copy.wait_send()
    for copy in cores:
        copy.wait_send()
    keep.wait()
    if flat is not None:
        flat_keep.start()
        for (row, _), copy in extra.items():
            if row >= 2:
                copy.wait_recv()
            copy.wait_send()
        flat_keep.wait()


def gather_kernel(depth, x_ref, table_ref, out_ref, tables_ref, send, recv, local):
    greet(depth)
    c = lax.axis_index("tensor")
    spread(depth, x_ref.at[c], out_ref, (send, recv), local.at[0], (table_ref, tables_ref))


def add_rows(rows, store, *terms):
    step = 16

    @pl.loop(0, rows // step)
    def _(i):
        at = pl.ds(pl.multiple_of(i * step, step), step)
        total = terms[0][at, :].astype(jnp.float32)
        for term in terms[1:]:
            total = total + term[at, :].astype(jnp.float32)
        store[at, :] = total.astype(store.dtype)


def reduce_kernel(
    depth, part_ref, out_ref, land_a, mine, send_b, land_b, send_c, land_c, own, total,
    rsend, rrecv, load, send, recv, local,
):
    d, z, c, first, second = place()
    rows = total.shape[0]
    order = list(range(1, depth)) + [0]
    loads = {}
    for k in order:
        zt = (z + k) % depth
        for slot, chip in ((1, second), (0, d)):
            loads[k, slot] = pltpu.make_async_copy(
                part_ref.at[chip * depth + zt], mine.at[k, slot], load.at[k, slot]
            )
            loads[k, slot].start()
    greet(depth)
    hop, turn, last = {}, {}, {}
    for k in order:
        zt = (z + k) % depth
        for slot, chip in ((1, 3 - d), (0, first)):
            hop[k, slot] = push(
                part_ref.at[chip * depth + zt], land_a.at[k, slot], (rsend, rrecv), slot, k, (first, z, c)
            )

    def finish(k):
        hop[k, 0].wait_recv()
        loads[k, 0].wait()
        turn[k].wait_recv()
        if k:
            add_rows(rows, send_c.at[k], mine.at[k, 0], land_a.at[k, 0], land_b.at[k])
            last[k] = push(
                send_c.at[k], land_c.at[k], (rsend, rrecv), 3, k, (d, (z + k) % depth, c)
            )
        else:
            add_rows(rows, own, mine.at[k, 0], land_a.at[k, 0], land_b.at[k])

    for i, k in enumerate(order):
        hop[k, 1].wait_recv()
        loads[k, 1].wait()
        add_rows(rows, send_b.at[k], mine.at[k, 1], land_a.at[k, 1])
        turn[k] = push(send_b.at[k], land_b.at[k], (rsend, rrecv), 2, k, (second, z, c))
        if i:
            finish(order[i - 1])
    finish(order[-1])
    for k in range(1, depth):
        last[k].wait_recv()
    add_rows(rows, total, own, *[land_c.at[k] for k in range(1, depth)])
    spread(depth, total, out_ref, (send, recv), local.at[0])
    for group in (hop, turn, last):
        for copy in group.values():
            copy.wait_send()


def gather_tokens(tokens, table):
    depth = lax.axis_size("expert")
    groups = lax.axis_size("dp") * depth
    count, width = tokens.shape
    half = count // 2
    dma = pltpu.SemaphoreType.DMA
    return pl.pallas_call(
        functools.partial(gather_kernel, depth),
        out_shape=(
            jax.ShapeDtypeStruct((groups, 2, half, width), jnp.bfloat16),
            jax.ShapeDtypeStruct((groups,) + table.shape, jnp.float32),
        ),
        in_specs=[ANY, ANY],
        out_specs=(ANY, ANY),
        scratch_shapes=[dma((12, depth)), dma((12, depth)), dma((1,))],
        compiler_params=pltpu.CompilerParams(
            collective_id=0, has_side_effects=True, vmem_limit_bytes=2 * 1024 * 1024
        ),
    )(tokens.reshape(2, half, width), table)


def reduce_and_spread(part):
    depth = lax.axis_size("expert")
    groups, rows, width = part.shape
    room = (8 * depth + 3) * rows * width * 2 + 4 * 1024 * 1024
    dma = pltpu.SemaphoreType.DMA
    buf = lambda *lead: pltpu.VMEM(lead + (rows, width), jnp.bfloat16)
    return pl.pallas_call(
        functools.partial(reduce_kernel, depth),
        out_shape=jax.ShapeDtypeStruct((groups, 2, rows, width), jnp.bfloat16),
        in_specs=[ANY],
        out_specs=ANY,
        scratch_shapes=[
            buf(depth, 2), buf(depth, 2), buf(depth), buf(depth), buf(depth), buf(depth),
            pltpu.VMEM((rows, width), jnp.float32), buf(),
            dma((4, depth)), dma((4, depth)), dma((depth, 2)),
            dma((8, depth)), dma((8, depth)), dma((1,)),
        ],
        compiler_params=pltpu.CompilerParams(
            collective_id=1, has_side_effects=True, vmem_limit_bytes=room
        ),
    )(part)


def body(tokens, expert_ids, gates, token_weight, w_gate, w_up, w_down, v_gate, v_up, v_down):
    tok_count, width = tokens.shape
    picks = expert_ids.shape[1]
    groups = lax.axis_size("dp") * lax.axis_size("expert")
    half_tok = tok_count // 2
    core = lax.axis_index("tensor")
    me = lax.axis_index("dp") * lax.axis_size("expert") + lax.axis_index("expert")
    labels = jnp.arange(groups, dtype=jnp.int32)
    dense = jnp.sum(
        jnp.where(expert_ids[:, :, None] == labels, gates[:, :, None], 0.0), axis=1
    )
    pad = -(groups + 1) % 8
    table = jnp.concatenate(
        [dense.T, token_weight[None], jnp.zeros((pad, tok_count), jnp.float32)], axis=0
    )
    x_parts, tables = gather_tokens(tokens, table)
    gate_of = lax.dynamic_index_in_dim(tables, me, 1, keepdims=False).reshape(-1, 1)
    scale_of = gate_of * tables[:, groups].reshape(-1, 1)
    down_mat, vdown_mat = w_down[0], v_down[0]
    x_parts, down_send, vdown_send = lax.optimization_barrier((x_parts, down_mat, vdown_mat))
    swap = [(0, 1), (1, 0)]
    down_other = lax.ppermute(down_send, "tensor", swap)
    vdown_other = lax.ppermute(vdown_send, "tensor", swap)
    mats = jnp.concatenate([down_mat, vdown_mat, down_other, vdown_other], axis=0)

    x = x_parts.reshape(groups * tok_count, width)
    pre_gate = product(x, w_gate[0])
    pre_up = product(x, w_up[0])
    d_gate = product(x, v_gate[0])
    d_up = product(x, v_up[0])
    silu_g, slope_g = silu_parts(pre_gate)
    act_wide = silu_g * pre_up
    act = act_wide.astype(jnp.bfloat16)
    d_act = (slope_g * d_gate * pre_up + silu_g * d_up).astype(jnp.bfloat16)

    hidden = act.shape[1]
    both = jnp.concatenate([d_act, act], axis=1).reshape(groups, 2, half_tok, 2 * hidden)
    keep = lax.dynamic_index_in_dim(both, core, 1, keepdims=False)
    give = lax.dynamic_index_in_dim(both, 1 - core, 1, keepdims=False)
    got = lax.ppermute(give, "tensor", swap)
    left = jnp.concatenate([keep, got], axis=2).reshape(groups * half_tok, 4 * hidden)
    gate_half = lax.dynamic_index_in_dim(
        gate_of.reshape(groups, 2, half_tok), core, 1, keepdims=False
    ).reshape(groups * half_tok, 1)
    part = (gate_half * product(left, mats)).astype(jnp.bfloat16)

    dy_parts = reduce_and_spread(part.reshape(groups, half_tok, width))
    dy = dy_parts.reshape(groups * tok_count, width)
    tangent = lax.dynamic_slice(
        dy, (me * tok_count, core * (width // 2)), (tok_count, width // 2)
    )
    back = scale_of * lax.dot_general(
        dy, w_down[0], (((1,), (1,)), ((), ())), preferred_element_type=jnp.float32
    )
    grad_gate = (back * pre_up * slope_g).astype(jnp.bfloat16)
    grad_up = (back * silu_g).astype(jnp.bfloat16)
    act_scaled = (scale_of * act_wide).astype(jnp.bfloat16)
    factor = 1.0 / (tok_count * picks) ** 0.5
    return (
        (factor * contract_rows(x, grad_gate))[None],
        (factor * contract_rows(x, grad_up))[None],
        (factor * contract_rows(act_scaled, dy))[None],
        tangent,
    )


def solution(mesh):
    rows = P(AXES, None)
    wide = P(AXES, None, "tensor")
    tall = P(AXES, "tensor", None)
    in_specs = (rows, rows, rows, P(AXES), wide, wide, tall, wide, wide, tall)
    out_specs = (wide, wide, tall, P(AXES, "tensor"))
    return jax.shard_map(body, mesh=mesh, in_specs=in_specs, out_specs=out_specs, check_vma=False)
```

```python
import functools

import jax
import jax.numpy as jnp
from jax import lax
from jax.experimental import pallas as pl
from jax.experimental.pallas import tpu as pltpu
from jax.sharding import PartitionSpec as P

MESH = pl.DeviceIdType.MESH
ANY = pl.BlockSpec(memory_space=pl.ANY)
AXES = ("dp", "expert")


def product(left, right):
    return jnp.dot(left, right, preferred_element_type=jnp.float32)


def contract_rows(left, right):
    return lax.dot_general(
        left, right, (((0,), (0,)), ((), ())), preferred_element_type=jnp.float32
    )


def silu_parts(pre_gate):
    sigma = jax.nn.sigmoid(pre_gate)
    return (pre_gate * sigma, sigma * (1.0 + pre_gate * (1.0 - sigma)))


def place():
    d, z, c = lax.axis_index("dp"), lax.axis_index("expert"), lax.axis_index("tensor")
    flip_low = d + 1 - 2 * (d % 2)
    flip_high = d + 2 - 4 * (d // 2)
    first = flip_low * (1 - c) + flip_high * c
    second = flip_high * (1 - c) + flip_low * c
    return d, z, c, first, second


def greet(depth):
    d, z, c, first, second = place()
    barrier = pltpu.get_barrier_semaphore()
    peers = [(d, (z + k) % depth, c) for k in range(1, depth)]
    peers += [(first, z, c), (second, z, c), (d, z, 1 - c)]
    for peer in peers:
        pl.semaphore_signal(barrier, inc=1, device_id=peer, device_id_type=MESH)
    pl.semaphore_wait(barrier, len(peers))


def push(src, dst, sems, row, col, peer):
    send, recv = sems
    copy = pltpu.make_async_remote_copy(
        src_ref=src, dst_ref=dst, send_sem=send.at[row, col], recv_sem=recv.at[row, col],
        device_id=peer, device_id_type=MESH,
    )
    copy.start()
    return copy


def spread(depth, src, out, sems, local_sem, small=None):
    d, z, c, first, second = place()
    to_first, to_second, to_core = (first, z, c), (second, z, c), (d, z, 1 - c)
    sent, along, one, two, three, cores = [], {}, {}, {}, {}, []
    spot = out.at[d * depth + z, c]
    keep = pltpu.make_async_copy(src, spot, local_sem)
    keep.start()
    extra, flat = {}, None
    if small is not None:
        flat, all_flat = small
        flat_spot = all_flat.at[d * depth + z]
        flat_keep = pltpu.make_async_copy(flat, flat_spot, local_sem)
    for k in range(1, depth):
        to_z = (d, (z + k) % depth, c)
        if flat is not None:
            extra[0, k] = push(flat, flat_spot, sems, 8, k, to_z)
        along[k] = push(src, spot, sems, 0, k, to_z)
    for j in range(depth + 1):
        if j < depth:
            from_z = (z - j + depth) % depth
            here = out.at[d * depth + from_z, c]
            if j:
                along[j].wait_recv()
            if flat is not None:
                if j:
                    extra[0, j].wait_recv()
                flat_here = all_flat.at[d * depth + from_z]
                flat_body = flat_here if j else flat
                extra[1, j] = push(flat_body, flat_here, sems, 9, j, to_first)
                extra[2, j] = push(flat_body, flat_here, sems, 10, j, to_second)
            body = here if j else src
            one[j] = push(body, here, sems, 1, j, to_first)
            two[j] = push(body, here, sems, 2, j, to_second)
            cores.append(push(body, here, sems, 4, j, to_core))
        if j >= 1:
            i = j - 1
            from_z = (z - i + depth) % depth
            one[i].wait_recv()
            here = out.at[first * depth + from_z, c]
            three[i] = push(here, here, sems, 3, i, to_second)
            if flat is not None:
                extra[1, i].wait_recv()
                flat_here = all_flat.at[first * depth + from_z]
                extra[3, i] = push(flat_here, flat_here, sems, 11, i, to_second)
            cores.append(push(here, here, sems, 5, i, to_core))
            two[i].wait_recv()
            here = out.at[second * depth + from_z, c]
            cores.append(push(here, here, sems, 6, i, to_core))
    for j in range(depth):
        from_z = (z - j + depth) % depth
        three[j].wait_recv()
        here = out.at[(3 - d) * depth + from_z, c]
        cores.append(push(here, here, sems, 7, j, to_core))
    for copy in cores:
        copy.wait_recv()
    for group in (along, one, two, three):
        for copy in group.values():
            copy.wait_send()
    for copy in cores:
        copy.wait_send()
    keep.wait()
    if flat is not None:
        flat_keep.start()
        for (row, _), copy in extra.items():
            if row >= 2:
                copy.wait_recv()
            copy.wait_send()
        flat_keep.wait()


def gather_kernel(depth, x_ref, table_ref, out_ref, tables_ref, send, recv, local):
    greet(depth)
    c = lax.axis_index("tensor")
    spread(depth, x_ref.at[c], out_ref, (send, recv), local.at[0], (table_ref, tables_ref))


def add_rows(rows, store, *terms):
    step = 16

    @pl.loop(0, rows // step)
    def _(i):
        at = pl.ds(pl.multiple_of(i * step, step), step)
        total = terms[0][at, :].astype(jnp.float32)
        for term in terms[1:]:
            total = total + term[at, :].astype(jnp.float32)
        store[at, :] = total.astype(store.dtype)


def reduce_kernel(
    depth, part_ref, out_ref, land_a, mine, send_b, land_b, send_c, land_c, own, total,
    rsend, rrecv, load, send, recv, local,
):
    d, z, c, first, second = place()
    rows = total.shape[0]
    order = list(range(1, depth)) + [0]
    loads = {}
    for k in order:
        zt = (z + k) % depth
        for slot, chip in ((1, second), (0, d)):
            loads[k, slot] = pltpu.make_async_copy(
                part_ref.at[chip * depth + zt], mine.at[k, slot], load.at[k, slot]
            )
            loads[k, slot].start()
    greet(depth)
    hop, turn, last = {}, {}, {}
    for k in order:
        zt = (z + k) % depth
        for slot, chip in ((1, 3 - d), (0, first)):
            hop[k, slot] = push(
                part_ref.at[chip * depth + zt], land_a.at[k, slot], (rsend, rrecv), slot, k, (first, z, c)
            )

    def finish(k):
        hop[k, 0].wait_recv()
        loads[k, 0].wait()
        turn[k].wait_recv()
        if k:
            add_rows(rows, send_c.at[k], mine.at[k, 0], land_a.at[k, 0], land_b.at[k])
            last[k] = push(
                send_c.at[k], land_c.at[k], (rsend, rrecv), 3, k, (d, (z + k) % depth, c)
            )
        else:
            add_rows(rows, own, mine.at[k, 0], land_a.at[k, 0], land_b.at[k])

    for i, k in enumerate(order):
        hop[k, 1].wait_recv()
        loads[k, 1].wait()
        add_rows(rows, send_b.at[k], mine.at[k, 1], land_a.at[k, 1])
        turn[k] = push(send_b.at[k], land_b.at[k], (rsend, rrecv), 2, k, (second, z, c))
        if i:
            finish(order[i - 1])
    finish(order[-1])
    for k in range(1, depth):
        last[k].wait_recv()
    add_rows(rows, total, own, *[land_c.at[k] for k in range(1, depth)])
    spread(depth, total, out_ref, (send, recv), local.at[0])
    for group in (hop, turn, last):
        for copy in group.values():
            copy.wait_send()


def gather_tokens(tokens, table):
    depth = lax.axis_size("expert")
    groups = lax.axis_size("dp") * depth
    count, width = tokens.shape
    half = count // 2
    dma = pltpu.SemaphoreType.DMA
    return pl.pallas_call(
        functools.partial(gather_kernel, depth),
        out_shape=(
            jax.ShapeDtypeStruct((groups, 2, half, width), jnp.bfloat16),
            jax.ShapeDtypeStruct((groups,) + table.shape, jnp.float32),
        ),
        in_specs=[ANY, ANY],
        out_specs=(ANY, ANY),
        scratch_shapes=[dma((12, depth)), dma((12, depth)), dma((1,))],
        compiler_params=pltpu.CompilerParams(
            collective_id=0, has_side_effects=True, vmem_limit_bytes=2 * 1024 * 1024
        ),
    )(tokens.reshape(2, half, width), table)


def reduce_and_spread(part):
    depth = lax.axis_size("expert")
    groups, rows, width = part.shape
    room = (8 * depth + 3) * rows * width * 2 + 4 * 1024 * 1024
    dma = pltpu.SemaphoreType.DMA
    buf = lambda *lead: pltpu.VMEM(lead + (rows, width), jnp.bfloat16)
    return pl.pallas_call(
        functools.partial(reduce_kernel, depth),
        out_shape=jax.ShapeDtypeStruct((groups, 2, rows, width), jnp.bfloat16),
        in_specs=[ANY],
        out_specs=ANY,
        scratch_shapes=[
            buf(depth, 2), buf(depth, 2), buf(depth), buf(depth), buf(depth), buf(depth),
            pltpu.VMEM((rows, width), jnp.float32), buf(),
            dma((4, depth)), dma((4, depth)), dma((depth, 2)),
            dma((8, depth)), dma((8, depth)), dma((1,)),
        ],
        compiler_params=pltpu.CompilerParams(
            collective_id=1, has_side_effects=True, vmem_limit_bytes=room
        ),
    )(part)


def forward_kernel(
    core_ref, x_ref, scale_ref, wg_ref, wu_ref, vg_ref, vu_ref,
    keep_ref, give_ref, act_ref, slope_ref, silu_ref, mats, held, sems,
):
    hidden = act_ref.shape[1]

    @pl.when(pl.program_id(0) == 0)
    def _():
        copies = [
            pltpu.make_async_copy(ref, mats.at[:, pl.ds(i * hidden, hidden)], sems.at[i])
            for i, ref in enumerate((wg_ref, wu_ref, vg_ref, vu_ref))
        ]
        for copy in copies:
            copy.start()
        for copy in copies:
            copy.wait()

    wide = product(x_ref[...], mats[...])
    pre_gate, pre_up, d_gate, d_up = (
        wide[:, i * hidden:(i + 1) * hidden] for i in range(4)
    )
    silu_g, slope_g = silu_parts(pre_gate)
    scale = scale_ref[...]
    act_wide = silu_g * pre_up
    up_slope = slope_g * pre_up
    shape = held.shape[:3] + (hidden,)
    d_act = (up_slope * d_gate + silu_g * d_up).astype(jnp.bfloat16)
    held[:, :, :, :hidden] = d_act.reshape(shape)
    held[:, :, :, hidden:] = act_wide.astype(jnp.bfloat16).reshape(shape)
    act_ref[...] = (scale * act_wide).astype(jnp.bfloat16)
    slope_ref[...] = scale * up_slope
    silu_ref[...] = scale * silu_g
    core = core_ref[0]
    keep_ref[...] = held[:, core]
    give_ref[...] = held[:, 1 - core]


def forward(core, x, scale, mats, groups, half_tok):
    count, width = x.shape
    hidden = mats[0].shape[1]
    tile = 256
    pair = tile // (2 * half_tok)
    flat = lambda cols: pl.BlockSpec((tile, cols), lambda i, core: (i, 0))
    part = pl.BlockSpec((pair, half_tok, 2 * hidden), lambda i, core: (i, 0, 0))
    row = lambda kind: jax.ShapeDtypeStruct((count, hidden), kind)
    piece = jax.ShapeDtypeStruct((groups, half_tok, 2 * hidden), jnp.bfloat16)
    return pl.pallas_call(
        forward_kernel,
        out_shape=(piece, piece, row(jnp.bfloat16), row(jnp.float32), row(jnp.float32)),
        grid_spec=pltpu.PrefetchScalarGridSpec(
            num_scalar_prefetch=1,
            grid=(count // tile,),
            in_specs=[flat(width), flat(1)] + [ANY] * 4,
            out_specs=(part, part, flat(hidden), flat(hidden), flat(hidden)),
            scratch_shapes=[
                pltpu.VMEM((width, 4 * hidden), jnp.bfloat16),
                pltpu.VMEM((pair, 2, half_tok, 2 * hidden), jnp.bfloat16),
                pltpu.SemaphoreType.DMA((4,)),
            ],
        ),
        compiler_params=pltpu.CompilerParams(vmem_limit_bytes=28 * 1024 * 1024),
        cost_estimate=pl.CostEstimate(
            flops=8 * count * width * hidden,
            bytes_accessed=2 * count * width + 8 * width * hidden + 20 * count * hidden,
            transcendentals=count * hidden,
        ),
    )(core, x, scale, *mats)


def body(tokens, expert_ids, gates, token_weight, w_gate, w_up, w_down, v_gate, v_up, v_down):
    tok_count, width = tokens.shape
    picks = expert_ids.shape[1]
    groups = lax.axis_size("dp") * lax.axis_size("expert")
    half_tok = tok_count // 2
    core = lax.axis_index("tensor")
    me = lax.axis_index("dp") * lax.axis_size("expert") + lax.axis_index("expert")
    labels = jnp.arange(groups, dtype=jnp.int32)
    dense = jnp.sum(
        jnp.where(expert_ids[:, :, None] == labels, gates[:, :, None], 0.0), axis=1
    )
    pad = -(groups + 1) % 8
    table = jnp.concatenate(
        [dense.T, token_weight[None], jnp.zeros((pad, tok_count), jnp.float32)], axis=0
    )
    x_parts, tables = gather_tokens(tokens, table)
    gate_of = lax.dynamic_index_in_dim(tables, me, 1, keepdims=False).reshape(-1, 1)
    scale_of = gate_of * tables[:, groups].reshape(-1, 1)
    down_mat, vdown_mat = w_down[0], v_down[0]
    x_parts, down_send, vdown_send = lax.optimization_barrier((x_parts, down_mat, vdown_mat))
    swap = [(0, 1), (1, 0)]
    down_other = lax.ppermute(down_send, "tensor", swap)
    vdown_other = lax.ppermute(vdown_send, "tensor", swap)
    mats = jnp.concatenate([down_mat, vdown_mat, down_other, vdown_other], axis=0)

    x = x_parts.reshape(groups * tok_count, width)
    keep, give, act_scaled, up_slope, silu_scaled = forward(
        core.reshape(1), x, scale_of, (w_gate[0], w_up[0], v_gate[0], v_up[0]), groups, half_tok
    )
    hidden = act_scaled.shape[1]
    got = lax.ppermute(give, "tensor", swap)
    left = jnp.concatenate([keep, got], axis=2).reshape(groups * half_tok, 4 * hidden)
    gate_half = lax.dynamic_index_in_dim(
        gate_of.reshape(groups, 2, half_tok), core, 1, keepdims=False
    ).reshape(groups * half_tok, 1)
    part = (gate_half * product(left, mats)).astype(jnp.bfloat16)

    dy_parts = reduce_and_spread(part.reshape(groups, half_tok, width))
    dy = dy_parts.reshape(groups * tok_count, width)
    tangent = lax.dynamic_slice(
        dy, (me * tok_count, core * (width // 2)), (tok_count, width // 2)
    )
    back = lax.dot_general(
        dy, w_down[0], (((1,), (1,)), ((), ())), preferred_element_type=jnp.float32
    )
    grad_gate = (back * up_slope).astype(jnp.bfloat16)
    grad_up = (back * silu_scaled).astype(jnp.bfloat16)
    factor = 1.0 / (tok_count * picks) ** 0.5
    return (
        (factor * contract_rows(x, grad_gate))[None],
        (factor * contract_rows(x, grad_up))[None],
        (factor * contract_rows(act_scaled, dy))[None],
        tangent,
    )


def solution(mesh):
    rows = P(AXES, None)
    wide = P(AXES, None, "tensor")
    tall = P(AXES, "tensor", None)
    in_specs = (rows, rows, rows, P(AXES), wide, wide, tall, wide, wide, tall)
    out_specs = (wide, wide, tall, P(AXES, "tensor"))
    return jax.shard_map(body, mesh=mesh, in_specs=in_specs, out_specs=out_specs, check_vma=False)
```

```python
import functools

import jax
import jax.numpy as jnp
from jax import lax
from jax.experimental import pallas as pl
from jax.experimental.pallas import tpu as pltpu
from jax.sharding import PartitionSpec as P

MESH = pl.DeviceIdType.MESH
ANY = pl.BlockSpec(memory_space=pl.ANY)
AXES = ("dp", "expert")


def product(left, right):
    return jnp.dot(left, right, preferred_element_type=jnp.float32)


def contract_rows(left, right):
    return lax.dot_general(
        left, right, (((0,), (0,)), ((), ())), preferred_element_type=jnp.float32
    )


def silu_parts(pre_gate):
    sigma = jax.nn.sigmoid(pre_gate)
    return (pre_gate * sigma, sigma * (1.0 + pre_gate * (1.0 - sigma)))


def place():
    d, z, c = lax.axis_index("dp"), lax.axis_index("expert"), lax.axis_index("tensor")
    flip_low = d + 1 - 2 * (d % 2)
    flip_high = d + 2 - 4 * (d // 2)
    first = flip_low * (1 - c) + flip_high * c
    second = flip_high * (1 - c) + flip_low * c
    return d, z, c, first, second


def greet(depth):
    d, z, c, first, second = place()
    barrier = pltpu.get_barrier_semaphore()
    peers = [(d, (z + k) % depth, c) for k in range(1, depth)]
    peers += [(first, z, c), (second, z, c), (d, z, 1 - c)]
    for peer in peers:
        pl.semaphore_signal(barrier, inc=1, device_id=peer, device_id_type=MESH)
    pl.semaphore_wait(barrier, len(peers))


def push(src, dst, sems, row, col, peer):
    send, recv = sems
    copy = pltpu.make_async_remote_copy(
        src_ref=src, dst_ref=dst, send_sem=send.at[row, col], recv_sem=recv.at[row, col],
        device_id=peer, device_id_type=MESH,
    )
    copy.start()
    return copy


def spread(depth, src, out, sems, local_sem, small=None):
    d, z, c, first, second = place()
    to_first, to_second, to_core = (first, z, c), (second, z, c), (d, z, 1 - c)
    sent, along, one, two, three, cores = [], {}, {}, {}, {}, []
    spot = out.at[d * depth + z, c]
    keep = pltpu.make_async_copy(src, spot, local_sem)
    keep.start()
    extra, flat = {}, None
    if small is not None:
        flat, all_flat = small
        flat_spot = all_flat.at[d * depth + z]
        flat_keep = pltpu.make_async_copy(flat, flat_spot, local_sem)
    for k in range(1, depth):
        to_z = (d, (z + k) % depth, c)
        if flat is not None:
            extra[0, k] = push(flat, flat_spot, sems, 8, k, to_z)
        along[k] = push(src, spot, sems, 0, k, to_z)
    for j in range(depth + 1):
        if j < depth:
            from_z = (z - j + depth) % depth
            here = out.at[d * depth + from_z, c]
            if j:
                along[j].wait_recv()
            if flat is not None:
                if j:
                    extra[0, j].wait_recv()
                flat_here = all_flat.at[d * depth + from_z]
                flat_body = flat_here if j else flat
                extra[1, j] = push(flat_body, flat_here, sems, 9, j, to_first)
                extra[2, j] = push(flat_body, flat_here, sems, 10, j, to_second)
            body = here if j else src
            one[j] = push(body, here, sems, 1, j, to_first)
            two[j] = push(body, here, sems, 2, j, to_second)
            cores.append(push(body, here, sems, 4, j, to_core))
        if j >= 1:
            i = j - 1
            from_z = (z - i + depth) % depth
            one[i].wait_recv()
            here = out.at[first * depth + from_z, c]
            three[i] = push(here, here, sems, 3, i, to_second)
            if flat is not None:
                extra[1, i].wait_recv()
                flat_here = all_flat.at[first * depth + from_z]
                extra[3, i] = push(flat_here, flat_here, sems, 11, i, to_second)
            cores.append(push(here, here, sems, 5, i, to_core))
            two[i].wait_recv()
            here = out.at[second * depth + from_z, c]
            cores.append(push(here, here, sems, 6, i, to_core))
    for j in range(depth):
        from_z = (z - j + depth) % depth
        three[j].wait_recv()
        here = out.at[(3 - d) * depth + from_z, c]
        cores.append(push(here, here, sems, 7, j, to_core))
    for copy in cores:
        copy.wait_recv()
    for group in (along, one, two, three):
        for copy in group.values():
            copy.wait_send()
    for copy in cores:
        copy.wait_send()
    keep.wait()
    if flat is not None:
        flat_keep.start()
        for (row, _), copy in extra.items():
            if row >= 2:
                copy.wait_recv()
            copy.wait_send()
        flat_keep.wait()


def gather_kernel(depth, x_ref, table_ref, out_ref, tables_ref, send, recv, local):
    greet(depth)
    c = lax.axis_index("tensor")
    spread(depth, x_ref.at[c], out_ref, (send, recv), local.at[0], (table_ref, tables_ref))


def add_rows(rows, store, *terms):
    step = 16

    @pl.loop(0, rows // step)
    def _(i):
        at = pl.ds(pl.multiple_of(i * step, step), step)
        total = terms[0][at, :].astype(jnp.float32)
        for term in terms[1:]:
            total = total + term[at, :].astype(jnp.float32)
        store[at, :] = total.astype(store.dtype)


def reduce_kernel(
    depth, part_ref, out_ref, land_a, mine, send_b, land_b, send_c, land_c, own, total,
    rsend, rrecv, load, send, recv, local,
):
    d, z, c, first, second = place()
    rows = total.shape[0]
    order = list(range(1, depth)) + [0]
    loads = {}
    for k in order:
        zt = (z + k) % depth
        for slot, chip in ((1, second), (0, d)):
            loads[k, slot] = pltpu.make_async_copy(
                part_ref.at[chip * depth + zt], mine.at[k, slot], load.at[k, slot]
            )
            loads[k, slot].start()
    greet(depth)
    hop, turn, last = {}, {}, {}
    for k in order:
        zt = (z + k) % depth
        for slot, chip in ((1, 3 - d), (0, first)):
            hop[k, slot] = push(
                part_ref.at[chip * depth + zt], land_a.at[k, slot], (rsend, rrecv), slot, k, (first, z, c)
            )

    def finish(k):
        hop[k, 0].wait_recv()
        loads[k, 0].wait()
        turn[k].wait_recv()
        if k:
            add_rows(rows, send_c.at[k], mine.at[k, 0], land_a.at[k, 0], land_b.at[k])
            last[k] = push(
                send_c.at[k], land_c.at[k], (rsend, rrecv), 3, k, (d, (z + k) % depth, c)
            )
        else:
            add_rows(rows, own, mine.at[k, 0], land_a.at[k, 0], land_b.at[k])

    for i, k in enumerate(order):
        hop[k, 1].wait_recv()
        loads[k, 1].wait()
        add_rows(rows, send_b.at[k], mine.at[k, 1], land_a.at[k, 1])
        turn[k] = push(send_b.at[k], land_b.at[k], (rsend, rrecv), 2, k, (second, z, c))
        if i:
            finish(order[i - 1])
    finish(order[-1])
    for k in range(1, depth):
        last[k].wait_recv()
    add_rows(rows, total, own, *[land_c.at[k] for k in range(1, depth)])
    spread(depth, total, out_ref, (send, recv), local.at[0])
    for group in (hop, turn, last):
        for copy in group.values():
            copy.wait_send()


def gather_tokens(tokens, table):
    depth = lax.axis_size("expert")
    groups = lax.axis_size("dp") * depth
    count, width = tokens.shape
    half = count // 2
    dma = pltpu.SemaphoreType.DMA
    return pl.pallas_call(
        functools.partial(gather_kernel, depth),
        out_shape=(
            jax.ShapeDtypeStruct((groups, 2, half, width), jnp.bfloat16),
            jax.ShapeDtypeStruct((groups,) + table.shape, jnp.float32),
        ),
        in_specs=[ANY, ANY],
        out_specs=(ANY, ANY),
        scratch_shapes=[dma((12, depth)), dma((12, depth)), dma((1,))],
        compiler_params=pltpu.CompilerParams(
            collective_id=0, has_side_effects=True, vmem_limit_bytes=60 * 1024 * 1024
        ),
        cost_estimate=pl.CostEstimate(
            flops=0, bytes_accessed=8 * groups * count * width, transcendentals=0
        ),
    )(tokens.reshape(2, half, width), table)


def reduce_and_spread(part):
    depth = lax.axis_size("expert")
    groups, rows, width = part.shape
    room = (8 * depth + 3) * rows * width * 2 + 4 * 1024 * 1024
    dma = pltpu.SemaphoreType.DMA
    buf = lambda *lead: pltpu.VMEM(lead + (rows, width), jnp.bfloat16)
    return pl.pallas_call(
        functools.partial(reduce_kernel, depth),
        out_shape=jax.ShapeDtypeStruct((groups, 2, rows, width), jnp.bfloat16),
        in_specs=[ANY],
        out_specs=ANY,
        scratch_shapes=[
            buf(depth, 2), buf(depth, 2), buf(depth), buf(depth), buf(depth), buf(depth),
            pltpu.VMEM((rows, width), jnp.float32), buf(),
            dma((4, depth)), dma((4, depth)), dma((depth, 2)),
            dma((8, depth)), dma((8, depth)), dma((1,)),
        ],
        compiler_params=pltpu.CompilerParams(
            collective_id=1, has_side_effects=True, vmem_limit_bytes=room
        ),
    )(part)


def forward_kernel(
    core_ref, x_ref, scale_ref, wg_ref, wu_ref, vg_ref, vu_ref,
    keep_ref, give_ref, act_ref, slope_ref, silu_ref, mats, held, sems,
):
    hidden = act_ref.shape[1]

    @pl.when(pl.program_id(0) == 0)
    def _():
        copies = [
            pltpu.make_async_copy(ref, mats.at[:, pl.ds(i * hidden, hidden)], sems.at[i])
            for i, ref in enumerate((wg_ref, wu_ref, vg_ref, vu_ref))
        ]
        for copy in copies:
            copy.start()
        for copy in copies:
            copy.wait()

    wide = product(x_ref[...], mats[...])
    pre_gate, pre_up, d_gate, d_up = (
        wide[:, i * hidden:(i + 1) * hidden] for i in range(4)
    )
    silu_g, slope_g = silu_parts(pre_gate)
    scale = scale_ref[...]
    act_wide = silu_g * pre_up
    up_slope = slope_g * pre_up
    shape = held.shape[:3] + (hidden,)
    d_act = (up_slope * d_gate + silu_g * d_up).astype(jnp.bfloat16)
    held[:, :, :, :hidden] = d_act.reshape(shape)
    held[:, :, :, hidden:] = act_wide.astype(jnp.bfloat16).reshape(shape)
    act_ref[...] = (scale * act_wide).astype(jnp.bfloat16)
    slope_ref[...] = scale * up_slope
    silu_ref[...] = scale * silu_g
    core = core_ref[0]
    keep_ref[...] = held[:, core]
    give_ref[...] = held[:, 1 - core]


def forward(core, x, scale, mats, groups, half_tok):
    count, width = x.shape
    hidden = mats[0].shape[1]
    tile = 256
    pair = tile // (2 * half_tok)
    flat = lambda cols: pl.BlockSpec((tile, cols), lambda i, core: (i, 0))
    part = pl.BlockSpec((pair, half_tok, 2 * hidden), lambda i, core: (i, 0, 0))
    row = lambda kind: jax.ShapeDtypeStruct((count, hidden), kind)
    piece = jax.ShapeDtypeStruct((groups, half_tok, 2 * hidden), jnp.bfloat16)
    return pl.pallas_call(
        forward_kernel,
        out_shape=(piece, piece, row(jnp.bfloat16), row(jnp.float32), row(jnp.float32)),
        grid_spec=pltpu.PrefetchScalarGridSpec(
            num_scalar_prefetch=1,
            grid=(count // tile,),
            in_specs=[flat(width), flat(1)] + [ANY] * 4,
            out_specs=(part, part, flat(hidden), flat(hidden), flat(hidden)),
            scratch_shapes=[
                pltpu.VMEM((width, 4 * hidden), jnp.bfloat16),
                pltpu.VMEM((pair, 2, half_tok, 2 * hidden), jnp.bfloat16),
                pltpu.SemaphoreType.DMA((4,)),
            ],
        ),
        compiler_params=pltpu.CompilerParams(vmem_limit_bytes=60 * 1024 * 1024),
        cost_estimate=pl.CostEstimate(
            flops=8 * count * width * hidden,
            bytes_accessed=2 * count * width + 8 * width * hidden + 20 * count * hidden,
            transcendentals=count * hidden,
        ),
    )(core, x, scale, *mats)


def body(tokens, expert_ids, gates, token_weight, w_gate, w_up, w_down, v_gate, v_up, v_down):
    tok_count, width = tokens.shape
    picks = expert_ids.shape[1]
    groups = lax.axis_size("dp") * lax.axis_size("expert")
    half_tok = tok_count // 2
    core = lax.axis_index("tensor")
    me = lax.axis_index("dp") * lax.axis_size("expert") + lax.axis_index("expert")
    labels = jnp.arange(groups, dtype=jnp.int32)
    dense = jnp.sum(
        jnp.where(expert_ids[:, :, None] == labels, gates[:, :, None], 0.0), axis=1
    )
    pad = -(groups + 1) % 8
    table = jnp.concatenate(
        [dense.T, token_weight[None], jnp.zeros((pad, tok_count), jnp.float32)], axis=0
    )
    x_parts, tables = gather_tokens(tokens, table)
    gate_of = lax.dynamic_index_in_dim(tables, me, 1, keepdims=False).reshape(-1, 1)
    scale_of = gate_of * tables[:, groups].reshape(-1, 1)
    down_mat, vdown_mat = w_down[0], v_down[0]
    swap = [(0, 1), (1, 0)]
    down_other = lax.ppermute(down_mat, "tensor", swap)
    vdown_other = lax.ppermute(vdown_mat, "tensor", swap)
    x_parts, down_other, vdown_other = lax.optimization_barrier(
        (x_parts, down_other, vdown_other)
    )
    mats = jnp.concatenate([down_mat, vdown_mat, down_other, vdown_other], axis=0)

    x = x_parts.reshape(groups * tok_count, width)
    keep, give, act_scaled, up_slope, silu_scaled = forward(
        core.reshape(1), x, scale_of, (w_gate[0], w_up[0], v_gate[0], v_up[0]), groups, half_tok
    )
    hidden = act_scaled.shape[1]
    got = lax.ppermute(give, "tensor", swap)
    left = jnp.concatenate([keep, got], axis=2).reshape(groups * half_tok, 4 * hidden)
    gate_half = lax.dynamic_index_in_dim(
        gate_of.reshape(groups, 2, half_tok), core, 1, keepdims=False
    ).reshape(groups * half_tok, 1)
    part = (gate_half * product(left, mats)).astype(jnp.bfloat16)

    dy_parts = reduce_and_spread(part.reshape(groups, half_tok, width))
    dy = dy_parts.reshape(groups * tok_count, width)
    tangent = lax.dynamic_slice(
        dy, (me * tok_count, core * (width // 2)), (tok_count, width // 2)
    )
    back = lax.dot_general(
        dy, w_down[0], (((1,), (1,)), ((), ())), preferred_element_type=jnp.float32
    )
    grad_gate = (back * up_slope).astype(jnp.bfloat16)
    grad_up = (back * silu_scaled).astype(jnp.bfloat16)
    factor = 1.0 / (tok_count * picks) ** 0.5
    return (
        (factor * contract_rows(x, grad_gate))[None],
        (factor * contract_rows(x, grad_up))[None],
        (factor * contract_rows(act_scaled, dy))[None],
        tangent,
    )


def solution(mesh):
    rows = P(AXES, None)
    wide = P(AXES, None, "tensor")
    tall = P(AXES, "tensor", None)
    in_specs = (rows, rows, rows, P(AXES), wide, wide, tall, wide, wide, tall)
    out_specs = (wide, wide, tall, P(AXES, "tensor"))
    return jax.shard_map(body, mesh=mesh, in_specs=in_specs, out_specs=out_specs, check_vma=False)
```
